32 devices in a mesh: front: 4 (over z), row: 4 (over y, core), col: 2 (over x).
Axes of the slice: x: 2, y: 2, z: 4, core: 2. Of those that a mesh axis runs over, the one named last changes fastest.
Arguments:
- pivot_block: float32 [8, 512, 512], P(('front', 'col'), 'row'), as said below
- panel_rows: float32 [8, 4096, 512], P(('front', 'col'), 'row'), may hold values from -0.875 to 0.875
- update_block: float32 [8, 4096, 4096], P(('front', 'col'), 'row'), as said below
- tile_map: int32 [8, 32], replicated, may hold values from 0 to 95, as said below
Outputs:
- pivot_factor: float32 [8, 512, 512], P(('front', 'col'), 'row')
- panel_factor: float32 [8, 4096, 512], P(('front', 'col'), 'row')
- parent_update: float32 [2, 12288, 12288], P('col', 'front', 'row')
The draws below stay inside these ranges and needn't reach their ends.
Inputs may be any that keep to these rules, and one draw needn't show every extreme that they name: `pivot_block`: each child's pivot block is symmetric positive definite. `update_block`: each child's update block is symmetric. `tile_map`: row c lists, strictly increasing, the parent tiles that receive child c's 32 tiles; child c belongs to parent c % 2. At most 9 entries of one row fall in any aligned block of 24 parent tiles, and exactly 9 do in some block.
All inputs are finite; a program needn't handle non-finite values.
Results may differ from the reference program's by a relative error of at most 0.0001.
Values sent between devices are 32-bit elements; how exact they have to be, the bound alone decides.
A program may use at most 192 MiB of HBM per device.

```python
import math
import jax
import jax.numpy as jnp
from jax import lax

PANEL = 512
TILE = 128
CONTRIB = 4096
PARENT = 12288
CHILDREN = 8
CTILES = 32
PTILES = 96
BLOCK = 24
N_COL = 2


def draw_pivot_block(key, part):

    def draw_child(subkey):
        key_jitter, key_diagonal = jax.random.split(subkey)
        spread_max = 1.8 / PANEL
        jitter = jax.random.uniform(key_jitter, (PANEL, PANEL), jnp.float32, -spread_max, spread_max)
        symmetric = 0.5 * (jitter + jitter.T)
        diagonal = jnp.exp(jax.random.uniform(key_diagonal, (PANEL,), jnp.float32, math.log(2.0), math.log(8.0)))
        identity = jnp.eye(PANEL, dtype=jnp.float32)
        return symmetric * (1.0 - identity) + identity * diagonal[None, :]
    return jax.vmap(draw_child)(jax.random.split(key, CHILDREN))


def draw_update_block(key, part):

    def draw_child(subkey):
        values = jax.random.normal(subkey, (CONTRIB, CONTRIB), jnp.float32)
        return 0.7071 * (values + values.T)
    return jax.vmap(draw_child)(jax.random.split(key, CHILDREN))


def draw_tile_map(key, part):
    blocks = PTILES // BLOCK
    base_count = CTILES // blocks
    key_hot, key_children = jax.random.split(key)
    hot_blocks = jax.random.randint(key_hot, (N_COL,), 0, blocks)

    def draw_child(subkey, child_index):
        key_partner, key_order, key_flip, key_within = jax.random.split(subkey, 4)
        hot_block = hot_blocks[child_index % N_COL]
        partner = (hot_block + 1 + jax.random.randint(key_partner, (), 0, blocks - 1)) % blocks
        block_ids = jnp.arange(blocks, dtype=jnp.int32)
        ranking = jax.random.permutation(key_order, blocks).astype(jnp.int32)
        pinned = ((block_ids == hot_block) | (block_ids == partner)).astype(jnp.int32)
        ordering = jnp.argsort(ranking + blocks * pinned)
        position = jnp.argsort(ordering).astype(jnp.int32)
        pair_total = (blocks - 2) // 2
        coin_flip = jax.random.randint(key_flip, (blocks,), 0, 2)
        in_pair = (position < 2 * pair_total) & (pinned == 0)
        parity = 1 - 2 * (position % 2)
        change = jnp.where(in_pair, parity * coin_flip[position // 2], 0)
        change = change + (block_ids == hot_block).astype(jnp.int32) - (block_ids == partner).astype(jnp.int32)
        counts = base_count + change
        within_rank = jax.vmap(lambda inner: jax.random.permutation(inner, BLOCK))(jax.random.split(key_within, blocks))
        chosen = (within_rank < counts[:, None]).reshape(-1)
        tile_ids = jnp.arange(PTILES, dtype=jnp.int32)
        return jnp.argsort(jnp.where(chosen, tile_ids, tile_ids + PTILES))[:CTILES].astype(jnp.int32)
    return jax.vmap(draw_child)(jax.random.split(key_children, CHILDREN), jnp.arange(CHILDREN, dtype=jnp.int32))


def level_of(key, dims, cuts, least, high):
    def one(dim, shards_of):
        heights = jax.random.uniform(jax.random.fold_in(jax.random.fold_in(key, 6), dim), (shards_of,), jnp.float32, least / len(cuts), high / len(cuts))
        return jnp.repeat(jnp.exp(heights), dims[dim] // shards_of).reshape((-1,) + (1,) * (len(dims) - dim - 1))

    level = one(*cuts[0])
    for cut in cuts[1:]:
        level = level * one(*cut)
    return level


def centred(stream_key, extent, width, reach, shards=(), held_as=jnp.bfloat16):
    gain = level_of(stream_key, extent, shards, -0.22, 0.18) if shards else 1.0
    entries = jax.random.normal(stream_key, extent, jnp.float32) * width * gain
    return jnp.minimum(jnp.maximum(entries, -reach), reach).astype(held_as)


def setup_inputs(seed: int = 0) -> dict:
    splits = jax.random.split(jax.random.key(seed), 5)
    pivot_block = draw_pivot_block(jax.random.fold_in(splits[4], 71), 0)
    panel_rows = centred(splits[1], (CHILDREN, CONTRIB, PANEL), 0.15, 0.875, ((0, 8), (1, 4)), jnp.float32)
    update_block = draw_update_block(jax.random.fold_in(splits[4], 71), 0)
    tile_map = draw_tile_map(jax.random.fold_in(splits[4], 71), 0)
    return dict(pivot_block=pivot_block, panel_rows=panel_rows, update_block=update_block, tile_map=tile_map)


def solve_panel(lower_factor, panel_block):
    return jax.scipy.linalg.solve_triangular(lower_factor, panel_block.T, lower=True).T

def reference(pivot_block, panel_rows, update_block, tile_map):
    lower_factor = jnp.linalg.cholesky(pivot_block)
    panel_factor = jax.vmap(solve_panel)(lower_factor, panel_rows)
    offsets = jnp.arange(TILE, dtype=jnp.int32)

    def add_child(child_index, parents):
        factor = lax.dynamic_index_in_dim(panel_factor, child_index, 0, keepdims=False)
        update = lax.dynamic_index_in_dim(update_block, child_index, 0, keepdims=False)
        contribution = update - jnp.dot(factor, factor.T, precision=lax.Precision.HIGHEST)
        tile_ids = lax.dynamic_index_in_dim(tile_map, child_index, 0, keepdims=False)
        positions = (tile_ids[:, None] * TILE + offsets[None, :]).reshape(-1).astype(jnp.int32)
        return parents.at[child_index % N_COL, positions[:, None], positions[None, :]].add(contribution)
    parents = lax.fori_loop(0, CHILDREN, add_child, jnp.zeros((N_COL, PARENT, PARENT), jnp.float32))
    return (lower_factor, panel_factor, parents)
```

```python
import functools

import jax
import jax.numpy as jnp
from jax import lax
from jax.experimental import pallas as pl
from jax.experimental.pallas import tpu as pltpu
from jax.sharding import PartitionSpec as P

TILE = 128
PARENT = 12288
GROUP = 4
HIGHEST = lax.Precision.HIGHEST
NT = (((1,), (1,)), ((), ()))
NN = (((1,), (0,)), ((), ()))


def mul(left, right, dims):
    return lax.dot_general(left, right, dims, precision=HIGHEST, preferred_element_type=jnp.float32)


def factor_tile(block):
    size = block.shape[0]
    row_ids = lax.broadcasted_iota(jnp.int32, (size, size), 0)
    col_ids = lax.broadcasted_iota(jnp.int32, (size, size), 1)
    inverse = (row_ids == col_ids).astype(jnp.float32)
    work = block
    scales = jnp.zeros((size, size), jnp.float32)
    for first in range(0, size, GROUP):
        base = first // 8 * 8
        tail = work[base:, :]
        tail_inverse = inverse[base:, :]
        rows_here = row_ids[base:, :]
        columns = [
            jnp.broadcast_to(tail[:, k : k + 1], tail.shape) for k in range(first, first + GROUP)
        ]
        for offset in range(GROUP):
            k = first + offset
            at = k - base
            column = columns[offset]
            pivot = column[at : at + 1, :]
            recip = 1.0 / pivot
            multiplier = jnp.where(rows_here > k, column * recip, 0.0)
            for later in range(offset + 1, GROUP):
                columns[later] = columns[later] - multiplier * columns[later][at : at + 1, :]
            tail_inverse = tail_inverse - multiplier * tail_inverse[at : at + 1, :]
            tail = tail - multiplier * tail[at : at + 1, :]
            scales = jnp.where(row_ids == k, lax.rsqrt(pivot), scales)
        if base:
            work = jnp.concatenate([work[:base, :], tail], axis=0)
            inverse = jnp.concatenate([inverse[:base, :], tail_inverse], axis=0)
        else:
            work, inverse = tail, tail_inverse
    upper = jnp.where(col_ids >= row_ids, work * scales, 0.0)
    return upper.T, inverse * scales


def pivot_kernel(pivot_ref, lower_ref, inverse_ref, work):
    size = pivot_ref.shape[0]
    blocks = size // TILE
    lower_ref[...] = jnp.zeros_like(lower_ref)
    inverse_ref[...] = jnp.zeros_like(inverse_ref)
    work[...] = pivot_ref[...]

    @pl.loop(0, blocks)
    def _(step):
        at = pl.ds(pl.multiple_of(step * TILE, TILE), TILE)
        lower, inverse = factor_tile(work[at, at])
        rows = lax.broadcasted_iota(jnp.int32, (size, TILE), 0)
        below = mul(work[:, at], inverse, NT)
        below = jnp.where(rows >= (step + 1) * TILE, below, 0.0)
        work[...] = work[...] - mul(below, below, NT)
        lower_ref[:, at] = below
        lower_ref[at, at] = lower
        inverse_ref[at, at] = inverse

    for block in range(1, blocks):
        lo, hi = block * TILE, (block + 1) * TILE
        partial = mul(lower_ref[lo:hi, :lo], inverse_ref[:lo, :lo], NN)
        inverse_ref[lo:hi, :lo] = -mul(inverse_ref[lo:hi, lo:hi], partial, NN)


def factor_pivot(pivot):
    size = pivot.shape[0]
    whole = pl.BlockSpec(memory_space=pltpu.VMEM)
    return pl.pallas_call(
        pivot_kernel,
        out_shape=[jax.ShapeDtypeStruct((size, size), jnp.float32)] * 2,
        in_specs=[whole],
        out_specs=[whole, whole],
        scratch_shapes=[pltpu.VMEM((size, size), jnp.float32)],
        compiler_params=pltpu.CompilerParams(vmem_limit_bytes=32 * 2**20),
        cost_estimate=pl.CostEstimate(flops=60 * 10**9, bytes_accessed=3 * 2**20, transcendentals=0),
        name="factor_pivot",
    )(pivot)


def split(value):
    high = value.astype(jnp.bfloat16)
    return high, (value - high.astype(jnp.float32)).astype(jnp.bfloat16)


def contribution_kernel(
    own_tiles, left_tiles, chunk, info, panel, own, halo, out, update, mine_high, mine_low, high, low, sems
):
    fronts = update.shape[0]
    width = update.shape[2]
    slots = width // TILE
    step = pl.program_id(0)
    mine_first = info[fronts]
    row_me = info[fronts + 1]

    @pl.when(step == 0)
    def _():
        for f in range(fronts):
            columns = pl.ds(pl.multiple_of(info[f] * TILE, TILE), width)
            for slot in range(slots):
                place = mine_first + slot - own_tiles * row_me
                inside = (place >= 0) & (place < own_tiles)
                target = update.at[f, pl.ds(slot * TILE, TILE), :]

                @pl.when(inside)
                def _():
                    rows = pl.ds(pl.multiple_of(place * TILE, TILE), TILE)
                    pltpu.make_async_copy(own.at[rows, columns], target, sems.at[f]).start()

                @pl.when(jnp.logical_not(inside))
                def _():
                    which = jnp.where(place < 0, -place - 1, left_tiles + place - own_tiles)
                    rows = pl.ds(pl.multiple_of(which * TILE, TILE), TILE)
                    pltpu.make_async_copy(halo.at[rows, columns], target, sems.at[f]).start()

        value = panel[pl.ds(pl.multiple_of(mine_first * TILE, TILE), width), :]
        mine_high[...], mine_low[...] = split(value)

    value = panel[pl.ds(pl.multiple_of(info[step] * TILE, TILE), width), :]
    high[...], low[...] = split(value)
    pltpu.make_async_copy(update.at[step], update.at[step], sems.at[step]).wait()

    def dot(left, right):
        return lax.dot_general(left, right, NT, preferred_element_type=jnp.float32)

    @pl.loop(0, slots // chunk)
    def _(part):
        at = pl.ds(pl.multiple_of(part * chunk * TILE, TILE), chunk * TILE)
        product = dot(high[...], mine_low[at, :]) + dot(low[...], mine_high[at, :])
        product = product + dot(high[...], mine_high[at, :])
        out[0, :, at] = update[step, at, :].T - product


def contribute(panel, own, halo, info, fronts, slots, own_tiles, left_tiles):
    width = slots * TILE
    depth = panel.shape[1]
    chunk = 3 if slots % 3 == 0 else 1
    return pl.pallas_call(
        functools.partial(contribution_kernel, own_tiles, left_tiles, chunk),
        out_shape=jax.ShapeDtypeStruct((fronts, width, width), jnp.float32),
        grid_spec=pltpu.PrefetchScalarGridSpec(
            num_scalar_prefetch=1,
            grid=(fronts,),
            in_specs=[
                pl.BlockSpec(memory_space=pltpu.VMEM),
                pl.BlockSpec(memory_space=pl.ANY),
                pl.BlockSpec(memory_space=pl.ANY),
            ],
            out_specs=pl.BlockSpec((1, width, width), lambda f, info: (f, 0, 0)),
            scratch_shapes=[
                pltpu.VMEM((fronts, width, width), jnp.float32),
                pltpu.VMEM((width, depth), jnp.bfloat16),
                pltpu.VMEM((width, depth), jnp.bfloat16),
                pltpu.VMEM((width, depth), jnp.bfloat16),
                pltpu.VMEM((width, depth), jnp.bfloat16),
                pltpu.SemaphoreType.DMA((fronts,)),
            ],
        ),
        compiler_params=pltpu.CompilerParams(vmem_limit_bytes=60 * 2**20),
        cost_estimate=pl.CostEstimate(
            flops=6 * fronts * width * width * depth, bytes_accessed=8 * fronts * width * width, transcendentals=0
        ),
        name="contribute",
    )(info, panel, own, halo)


def assemble_kernel(fronts, slots, fetch, valid, target, *refs):
    blocks, out = refs[:fronts], refs[fronts]
    here = pl.program_id(0)
    out[...] = jnp.zeros_like(out)
    for k in range(fronts):

        @pl.when(valid[k, here] > 0)
        def _():
            for slot in range(slots):
                place = target[k, slot]

                @pl.when(place >= 0)
                def _():
                    at = pl.ds(pl.multiple_of(place * TILE, TILE), TILE)
                    out[:, at] = out[:, at] + blocks[k][0, :, slot * TILE : (slot + 1) * TILE]


def assemble(routed, fetch, valid, target, block_width):
    fronts, width, _ = routed.shape
    slots = width // TILE
    order = block_width * TILE

    def spec(k):
        return pl.BlockSpec((1, TILE, width), lambda a, fetch, valid, target: (k, fetch[k, a], 0))

    return pl.pallas_call(
        functools.partial(assemble_kernel, fronts, slots),
        out_shape=jax.ShapeDtypeStruct((order, order), jnp.float32),
        grid_spec=pltpu.PrefetchScalarGridSpec(
            num_scalar_prefetch=3,
            grid=(block_width,),
            in_specs=[spec(k) for k in range(fronts)],
            out_specs=pl.BlockSpec((TILE, order), lambda a, fetch, valid, target: (a, 0)),
        ),
        compiler_params=pltpu.CompilerParams(vmem_limit_bytes=48 * 2**20),
        cost_estimate=pl.CostEstimate(
            flops=0, bytes_accessed=4 * (fronts * width * width + order * order), transcendentals=0
        ),
        name="assemble",
    )(fetch, valid, target, *([routed] * fronts))


def exchange_halo(own, row_count, own_tiles, slots, tiles):
    left, right = [], []
    for r in range(row_count):
        left.append(own_tiles * r - max(0, tiles - slots * (row_count - r)))
        right.append(min(tiles, slots * (r + 1)) - own_tiles * (r + 1))

    def tile_row(index):
        return lax.slice_in_dim(own, index * TILE, (index + 1) * TILE, axis=0)

    pieces = []
    for t in range(1, max(left) + 1):
        distance = (t + own_tiles - 1) // own_tiles
        pairs = [(r - distance, r) for r in range(row_count) if left[r] >= t]
        pieces.append(lax.ppermute(tile_row(-t % own_tiles), "row", pairs))
    for t in range(max(right)):
        distance = 1 + t // own_tiles
        pairs = [(r + distance, r) for r in range(row_count) if right[r] > t]
        pieces.append(lax.ppermute(tile_row(t % own_tiles), "row", pairs))
    return jnp.concatenate(pieces, axis=0), max(left)


def local(pivot_block, panel_rows, update_block, tile_map):
    row_count = lax.axis_size("row")
    front_count = lax.axis_size("front")
    col_count = lax.axis_size("col")
    row_me = lax.axis_index("row")
    front_me = lax.axis_index("front")
    col_me = lax.axis_index("col")
    pivot_share = pivot_block.shape[1]
    own_rows = panel_rows.shape[1]
    tiles = update_block.shape[2] // TILE
    own_tiles = own_rows // TILE
    row_width = PARENT // TILE // row_count
    slots = tiles // row_count + 1

    pivot_whole = lax.all_gather(pivot_block[0], "row", axis=0, tiled=True)
    panel_whole = lax.all_gather(panel_rows[0], "row", axis=0, tiled=True)
    halo, left_tiles = exchange_halo(update_block[0], row_count, own_tiles, slots, tiles)

    def first_tile(maps, block):
        count = jnp.sum((maps // row_width < block).astype(jnp.int32), axis=-1)
        return jnp.minimum(count, tiles - slots)

    child_map = lax.dynamic_index_in_dim(tile_map, front_me * col_count + col_me, 0, keepdims=False)
    block_ids = jnp.arange(front_count, dtype=jnp.int32)
    info = jnp.concatenate(
        [
            first_tile(child_map[None, :], block_ids[:, None]),
            jnp.stack([first_tile(child_map, row_me), row_me]).astype(jnp.int32),
        ]
    )
    sources = jnp.arange(front_count, dtype=jnp.int32) * col_count + col_me
    maps = jnp.take(tile_map, sources, axis=0)
    slot_ids = jnp.arange(slots, dtype=jnp.int32)[None, :]
    row_first = first_tile(maps, front_me)[:, None]
    picked = jnp.take_along_axis(maps, row_first + slot_ids, axis=1) - front_me * row_width
    places = jnp.arange(row_width, dtype=jnp.int32)
    hit = picked[:, :, None] == places[None, None, :]
    valid = jnp.any(hit, axis=1).astype(jnp.int32)
    reached = jnp.sum((picked[:, :, None] <= places[None, None, :]).astype(jnp.int32), axis=1)
    fetch = jnp.clip(reached - 1, 0, slots - 1)
    col_first = first_tile(maps, row_me)[:, None]
    target = jnp.take_along_axis(maps, col_first + slot_ids, axis=1) - row_me * row_width
    target = jnp.where((target >= 0) & (target < row_width), target, -1)

    lower, inverse = factor_pivot(pivot_whole)
    panel = mul(panel_whole, inverse, NT)
    source = contribute(
        panel, update_block[0], halo, info, front_count, slots, own_tiles, left_tiles
    )
    routed = lax.all_to_all(source, "front", split_axis=0, concat_axis=0, tiled=True)
    parent = assemble(routed, fetch, valid, target, row_width)
    lower_own = lax.dynamic_slice_in_dim(lower, row_me * pivot_share, pivot_share, 0)
    panel_own = lax.dynamic_slice_in_dim(panel, row_me * own_rows, own_rows, 0)
    return (lower_own[None], panel_own[None], parent[None])


def solution(mesh):
    return jax.shard_map(
        local,
        mesh=mesh,
        in_specs=(
            P(("front", "col"), "row", None),
            P(("front", "col"), "row", None),
            P(("front", "col"), "row", None),
            P(),
        ),
        out_specs=(
            P(("front", "col"), "row", None),
            P(("front", "col"), "row", None),
            P("col", "front", "row"),
        ),
        check_vma=False,
    )
```

```python
import functools

import jax
import jax.numpy as jnp
from jax import lax
from jax.experimental import pallas as pl
from jax.experimental.pallas import tpu as pltpu
from jax.sharding import PartitionSpec as P

TILE = 128
PARENT = 12288
GROUP = 4
HIGHEST = lax.Precision.HIGHEST
NT = (((1,), (1,)), ((), ()))
NN = (((1,), (0,)), ((), ()))


def mul(left, right, dims):
    return lax.dot_general(left, right, dims, precision=HIGHEST, preferred_element_type=jnp.float32)


def factor_tile(block):
    size = block.shape[0]
    row_ids = lax.broadcasted_iota(jnp.int32, (size, size), 0)
    col_ids = lax.broadcasted_iota(jnp.int32, (size, size), 1)
    inverse = (row_ids == col_ids).astype(jnp.float32)
    work = block
    scales = jnp.zeros((size, size), jnp.float32)
    for first in range(0, size, GROUP):
        base = first // 8 * 8
        tail = work[base:, :]
        tail_inverse = inverse[base:, :]
        rows_here = row_ids[base:, :]
        columns = [
            jnp.broadcast_to(tail[:, k : k + 1], tail.shape) for k in range(first, first + GROUP)
        ]
        for offset in range(GROUP):
            k = first + offset
            at = k - base
            column = columns[offset]
            pivot = column[at : at + 1, :]
            recip = 1.0 / pivot
            multiplier = jnp.where(rows_here > k, column * recip, 0.0)
            for later in range(offset + 1, GROUP):
                columns[later] = columns[later] - multiplier * columns[later][at : at + 1, :]
            tail_inverse = tail_inverse - multiplier * tail_inverse[at : at + 1, :]
            tail = tail - multiplier * tail[at : at + 1, :]
            scales = jnp.where(row_ids == k, lax.rsqrt(pivot), scales)
        if base:
            work = jnp.concatenate([work[:base, :], tail], axis=0)
            inverse = jnp.concatenate([inverse[:base, :], tail_inverse], axis=0)
        else:
            work, inverse = tail, tail_inverse
    upper = jnp.where(col_ids >= row_ids, work * scales, 0.0)
    return upper.T, inverse * scales


def pivot_kernel(pivot_ref, lower_ref, inverse_ref, work):
    size = pivot_ref.shape[0]
    blocks = size // TILE
    lower_ref[...] = jnp.zeros_like(lower_ref)
    inverse_ref[...] = jnp.zeros_like(inverse_ref)
    work[...] = pivot_ref[...]

    @pl.loop(0, blocks)
    def _(step):
        at = pl.ds(pl.multiple_of(step * TILE, TILE), TILE)
        lower, inverse = factor_tile(work[at, at])
        rows = lax.broadcasted_iota(jnp.int32, (size, TILE), 0)
        below = mul(work[:, at], inverse, NT)
        below = jnp.where(rows >= (step + 1) * TILE, below, 0.0)
        work[...] = work[...] - mul(below, below, NT)
        lower_ref[:, at] = below
        lower_ref[at, at] = lower
        inverse_ref[at, at] = inverse

    for block in range(1, blocks):
        lo, hi = block * TILE, (block + 1) * TILE
        partial = mul(lower_ref[lo:hi, :lo], inverse_ref[:lo, :lo], NN)
        inverse_ref[lo:hi, :lo] = -mul(inverse_ref[lo:hi, lo:hi], partial, NN)


def factor_pivot(pivot):
    size = pivot.shape[0]
    whole = pl.BlockSpec(memory_space=pltpu.VMEM)
    return pl.pallas_call(
        pivot_kernel,
        out_shape=[jax.ShapeDtypeStruct((size, size), jnp.float32)] * 2,
        in_specs=[whole],
        out_specs=[whole, whole],
        scratch_shapes=[pltpu.VMEM((size, size), jnp.float32)],
        compiler_params=pltpu.CompilerParams(vmem_limit_bytes=32 * 2**20),
        cost_estimate=pl.CostEstimate(flops=60 * 10**9, bytes_accessed=3 * 2**20, transcendentals=0),
        name="factor_pivot",
    )(pivot)


def split(value):
    high = value.astype(jnp.bfloat16)
    return high, (value - high.astype(jnp.float32)).astype(jnp.bfloat16)


def contribution_kernel(own_tiles, left_tiles, first_slot, pieces, info, panel, own, *refs):
    halo, (out, update, mine_high, mine_low, high, low, sems) = refs[:pieces], refs[-7:]
    fronts, mine_width, width = update.shape
    step = pl.program_id(0)
    mine_first = info[fronts] + first_slot
    row_me = info[fronts + 1]

    @pl.when(step == 0)
    def _():
        for f in range(fronts):
            columns = pl.ds(pl.multiple_of(info[f] * TILE, TILE), width)
            for slot in range(mine_width // TILE):
                place = mine_first + slot - own_tiles * row_me
                target = update.at[f, pl.ds(slot * TILE, TILE), :]

                @pl.when((place >= 0) & (place < own_tiles))
                def _():
                    rows = pl.ds(pl.multiple_of(place * TILE, TILE), TILE)
                    pltpu.make_async_copy(own.at[rows, columns], target, sems.at[f]).start()

                for piece in range(pieces):
                    at = -piece - 1 if piece < left_tiles else own_tiles + piece - left_tiles

                    @pl.when(place == at)
                    def _():
                        pltpu.make_async_copy(halo[piece].at[:, columns], target, sems.at[f]).start()

        value = panel[pl.ds(pl.multiple_of(mine_first * TILE, TILE), mine_width), :]
        mine_high[...], mine_low[...] = split(value)

    value = panel[pl.ds(pl.multiple_of(info[step] * TILE, TILE), width), :]
    high[...], low[...] = split(value)
    pltpu.make_async_copy(update.at[step], update.at[step], sems.at[step]).wait()

    def dot(left, right):
        return lax.dot_general(left, right, NT, preferred_element_type=jnp.float32)

    product = dot(high[...], mine_low[...]) + dot(low[...], mine_high[...])
    product = product + dot(high[...], mine_high[...])
    out[0] = update[step].T - product


def contribute(panel, own, halo, after, info, fronts, slots, first_slot, chunk, own_tiles, left_tiles):
    width = slots * TILE
    mine_width = chunk * TILE
    depth = panel.shape[1]
    anywhere = pl.BlockSpec(memory_space=pl.ANY)
    return pl.pallas_call(
        functools.partial(contribution_kernel, own_tiles, left_tiles, first_slot, len(halo)),
        out_shape=jax.ShapeDtypeStruct((fronts, width, mine_width), jnp.float32),
        grid_spec=pltpu.PrefetchScalarGridSpec(
            num_scalar_prefetch=1,
            grid=(fronts,),
            in_specs=[pl.BlockSpec(memory_space=pltpu.VMEM)] + [anywhere] * (1 + len(halo) + len(after)),
            out_specs=pl.BlockSpec((1, width, mine_width), lambda f, info: (f, 0, 0)),
            scratch_shapes=[
                pltpu.VMEM((fronts, mine_width, width), jnp.float32),
                pltpu.VMEM((mine_width, depth), jnp.bfloat16),
                pltpu.VMEM((mine_width, depth), jnp.bfloat16),
                pltpu.VMEM((width, depth), jnp.bfloat16),
                pltpu.VMEM((width, depth), jnp.bfloat16),
                pltpu.SemaphoreType.DMA((fronts,)),
            ],
        ),
        compiler_params=pltpu.CompilerParams(vmem_limit_bytes=44 * 2**20),
        cost_estimate=pl.CostEstimate(
            flops=6 * fronts * width * mine_width * depth,
            bytes_accessed=8 * fronts * width * mine_width,
            transcendentals=0,
        ),
        name="contribute",
    )(info, panel, own, *halo, *after)


def assemble_kernel(fronts, firsts, fetch, valid, target, *refs):
    blocks, out = refs[:-1], refs[-1]
    here = pl.program_id(0)
    out[...] = jnp.zeros_like(out)
    for k in range(fronts):

        @pl.when(valid[k, here] > 0)
        def _():
            for part, first in enumerate(firsts):
                block = blocks[part * fronts + k]
                for slot in range(block.shape[2] // TILE):
                    place = target[k, first + slot]

                    @pl.when(place >= 0)
                    def _():
                        at = pl.ds(pl.multiple_of(place * TILE, TILE), TILE)
                        out[:, at] = out[:, at] + block[0, :, slot * TILE : (slot + 1) * TILE]


def assemble(parts, firsts, fetch, valid, target, block_width):
    fronts, width, part_width = parts[0].shape
    order = block_width * TILE

    def spec(k):
        return pl.BlockSpec((1, TILE, part_width), lambda a, fetch, valid, target: (k, fetch[k, a], 0))

    return pl.pallas_call(
        functools.partial(assemble_kernel, fronts, firsts),
        out_shape=jax.ShapeDtypeStruct((order, order), jnp.float32),
        grid_spec=pltpu.PrefetchScalarGridSpec(
            num_scalar_prefetch=3,
            grid=(block_width,),
            in_specs=[spec(k) for _ in parts for k in range(fronts)],
            out_specs=pl.BlockSpec((TILE, order), lambda a, fetch, valid, target: (a, 0)),
        ),
        compiler_params=pltpu.CompilerParams(vmem_limit_bytes=48 * 2**20),
        cost_estimate=pl.CostEstimate(
            flops=0, bytes_accessed=4 * (fronts * width * width + order * order), transcendentals=0
        ),
        name="assemble",
    )(fetch, valid, target, *[part for part in parts for _ in range(fronts)])


def exchange_halo(own, later, row_count, own_tiles, slots, tiles):
    left, right = [], []
    for r in range(row_count):
        left.append(own_tiles * r - max(0, tiles - slots * (row_count - r)))
        right.append(min(tiles, slots * (r + 1)) - own_tiles * (r + 1))

    def tile_row(index):
        return lax.slice_in_dim(own, index * TILE, (index + 1) * TILE, axis=0) + later

    pieces = []
    for t in range(1, max(left) + 1):
        distance = (t + own_tiles - 1) // own_tiles
        pairs = [(r - distance, r) for r in range(row_count) if left[r] >= t]
        pieces.append(lax.ppermute(tile_row(-t % own_tiles), "row", pairs))
    for t in range(max(right)):
        distance = 1 + t // own_tiles
        pairs = [(r + distance, r) for r in range(row_count) if right[r] > t]
        pieces.append(lax.ppermute(tile_row(t % own_tiles), "row", pairs))
    return pieces, max(left)


def always_own(row_count, own_tiles, slots, tiles, first_slot, chunk):
    for r in range(row_count):
        least = max(0, tiles - slots * (row_count - r)) + first_slot - own_tiles * r
        most = min(tiles - slots, slots * r) + first_slot + chunk - 1 - own_tiles * r
        if least < 0 or most >= own_tiles:
            return False
    return True


def local(pivot_block, panel_rows, update_block, tile_map):
    row_count = lax.axis_size("row")
    front_count = lax.axis_size("front")
    col_count = lax.axis_size("col")
    row_me = lax.axis_index("row")
    front_me = lax.axis_index("front")
    col_me = lax.axis_index("col")
    pivot_share = pivot_block.shape[1]
    own_rows = panel_rows.shape[1]
    tiles = update_block.shape[2] // TILE
    own_tiles = own_rows // TILE
    row_width = PARENT // TILE // row_count
    slots = tiles // row_count + 1

    pivot_whole = lax.all_gather(pivot_block[0], "row", axis=0, tiled=True)
    panel_whole = lax.all_gather(panel_rows[0], "row", axis=0, tiled=True)
    def first_tile(maps, block):
        count = jnp.sum((maps // row_width < block).astype(jnp.int32), axis=-1)
        return jnp.minimum(count, tiles - slots)

    child_map = lax.dynamic_index_in_dim(tile_map, front_me * col_count + col_me, 0, keepdims=False)
    block_ids = jnp.arange(front_count, dtype=jnp.int32)
    info = jnp.concatenate(
        [
            first_tile(child_map[None, :], block_ids[:, None]),
            jnp.stack([first_tile(child_map, row_me), row_me]).astype(jnp.int32),
        ]
    )
    sources = jnp.arange(front_count, dtype=jnp.int32) * col_count + col_me
    maps = jnp.take(tile_map, sources, axis=0)
    slot_ids = jnp.arange(slots, dtype=jnp.int32)[None, :]
    row_first = first_tile(maps, front_me)[:, None]
    picked = jnp.take_along_axis(maps, row_first + slot_ids, axis=1) - front_me * row_width
    places = jnp.arange(row_width, dtype=jnp.int32)
    hit = picked[:, :, None] == places[None, None, :]
    valid = jnp.any(hit, axis=1).astype(jnp.int32)
    reached = jnp.sum((picked[:, :, None] <= places[None, None, :]).astype(jnp.int32), axis=1)
    fetch = jnp.clip(reached - 1, 0, slots - 1)
    col_first = first_tile(maps, row_me)[:, None]
    target = jnp.take_along_axis(maps, col_first + slot_ids, axis=1) - row_me * row_width
    target = jnp.where((target >= 0) & (target < row_width), target, -1)

    lower, inverse = factor_pivot(pivot_whole)
    later = 0.0 * inverse[0, 0]
    halo, left_tiles = exchange_halo(update_block[0], later, row_count, own_tiles, slots, tiles)
    panel = mul(panel_whole, inverse, NT)
    chunk = slots // 3 if slots % 3 == 0 else slots
    firsts = list(range(0, slots, chunk))
    if len(firsts) == 3:
        firsts = [firsts[1], firsts[0], firsts[2]]
    parts, after = [], []
    for first_slot in firsts:
        inner = always_own(row_count, own_tiles, slots, tiles, first_slot, chunk)
        source = contribute(
            panel,
            update_block[0],
            [] if inner else halo,
            after,
            info,
            front_count,
            slots,
            first_slot,
            chunk,
            own_tiles,
            left_tiles,
        )
        after = [source]
        parts.append(lax.all_to_all(source, "front", split_axis=0, concat_axis=0, tiled=True))
    parent = assemble(parts, firsts, fetch, valid, target, row_width)
    lower_own = lax.dynamic_slice_in_dim(lower, row_me * pivot_share, pivot_share, 0)
    panel_own = lax.dynamic_slice_in_dim(panel, row_me * own_rows, own_rows, 0)
    return (lower_own[None], panel_own[None], parent[None])


def solution(mesh):
    return jax.shard_map(
        local,
        mesh=mesh,
        in_specs=(
            P(("front", "col"), "row", None),
            P(("front", "col"), "row", None),
            P(("front", "col"), "row", None),
            P(),
        ),
        out_specs=(
            P(("front", "col"), "row", None),
            P(("front", "col"), "row", None),
            P("col", "front", "row"),
        ),
        check_vma=False,
    )
```
